32 devices in a mesh: aux: 8 (over z, x), pair: 4 (over y, core).
Axes of the slice: x: 2, y: 2, z: 4, core: 2. Of those that a mesh axis runs over, the one named last changes fastest.
Arguments:
- three_centre: bfloat16 [16, 160, 128, 128], P('pair', 'aux'), may hold values from -6 to 6
- block_mask: int32 [16], replicated, may hold values from 0 to 1, as said below
- block_owner: int32 [16], replicated, may hold values from 0 to 3, as said below
- block_index: int32 [2, 16], replicated, may hold values from 0 to 23
- active_orbitals: bfloat16 [24, 3072], replicated, may hold values from -0.5 to 0.5
- inactive_orbitals: bfloat16 [256, 3072], replicated, may hold values from -0.75 to 0.75
Outputs:
- fock_blocks: float32 [32, 128, 128], P('pair')
- active_integrals: float32 [576, 576], P('aux')
The draws below stay inside these ranges and needn't reach their ends.
Inputs may be any that keep to these rules, and one draw needn't show every extreme that they name: `block_mask`: every index of pair holds at least 2 live slots. `block_owner`: among the 4 slots of one index of pair, live or not, at most 2 name any one owner; one owner is named by exactly 2 live slots of every index of pair, so it receives 8 live blocks.
All inputs are finite; a program needn't handle non-finite values.
Results may differ from the reference program's by a relative error of at most 0.0044.
Values may be sent and summed in bfloat16 or wider, within the bound.
A program may use at most 64 MiB of HBM per device.

```python
import math
import jax
import jax.numpy as jnp
from jax import lax

NAO = 3072
BW = 128
NB = 24
ACT = 24
PAIRS = 576
NIN = 256
AUX = 160
SLOT_IN = 4
SLOTS = 16
OWN = 8
N_PAIR = 4


def owner_plan(key):
    capacity = SLOT_IN // 2
    hottest = jax.random.randint(jax.random.fold_in(key, 11), (), 0, N_PAIR)
    owner_parts = []
    mask_parts = []
    for source in range(N_PAIR):
        source_key = jax.random.fold_in(key, 100 + source)
        ticket_key, live_key, order_key = jax.random.split(source_key, 3)
        tickets = jax.random.permutation(ticket_key, (N_PAIR - 1) * capacity)[:SLOT_IN - capacity] // capacity
        others = (hottest + 1 + tickets) % N_PAIR
        sequence = jnp.concatenate([jnp.full((capacity,), hottest, jnp.int32), others.astype(jnp.int32)])
        living = jnp.concatenate([jnp.ones((capacity,), jnp.int32), jax.random.randint(live_key, (SLOT_IN - capacity,), 0, 2).astype(jnp.int32)])
        ordering = jax.random.permutation(order_key, SLOT_IN)
        owner_parts.append(sequence[ordering])
        mask_parts.append(living[ordering])
    return (jnp.concatenate(owner_parts).astype(jnp.int32), jnp.concatenate(mask_parts).astype(jnp.int32))


def draw_block_mask(key, part):
    return owner_plan(jax.random.fold_in(key, 7))[1]


def draw_block_owner(key, part):
    return owner_plan(jax.random.fold_in(key, 7))[0]


def touch_ends(array, own_key, least, top_value):
    longest = array.shape.index(max(array.shape))
    spots = []
    for shift in (0, 1):
        where = [jax.random.randint(jax.random.fold_in(own_key, axis), (), 0, length) for axis, length in enumerate(array.shape)]
        where[longest] = (where[longest] + shift) % array.shape[longest]
        spots.append(tuple(where))
    return array.at[spots[0]].set(least).at[spots[1]].set(top_value)


def block_scale(stream_key, extent, cuts, low, top_value):
    def one(axis_at, parts):
        steps = jax.random.uniform(jax.random.fold_in(jax.random.fold_in(stream_key, 6), axis_at), (parts,), jnp.float32, low / len(cuts), top_value / len(cuts))
        return jnp.repeat(jnp.exp(steps), extent[axis_at] // parts).reshape((-1,) + (1,) * (len(extent) - axis_at - 1))

    loudness = one(*cuts[0])
    for cut in cuts[1:]:
        loudness = loudness * one(*cut)
    return loudness


def centred(key, shape, deviation, reach, shards=(), held_as=jnp.bfloat16):
    result = jax.random.normal(key, shape, jnp.float32) * deviation
    if len(shards) > 0:
        result = block_scale(key, shape, shards, -0.22, 0.18) * result
    return jnp.clip(result, min=-reach, max=reach).astype(held_as)


def setup_inputs(seed: int = 0) -> dict:
    arg_keys = jax.random.split(jax.random.key(seed), 7)
    three_centre = centred(arg_keys[0], (SLOTS, AUX, BW, BW), 1.0, 6.0, ((0, 4), (1, 8)))
    block_mask = draw_block_mask(jax.random.fold_in(arg_keys[6], 71), 0)
    block_owner = draw_block_owner(jax.random.fold_in(arg_keys[6], 71), 0)
    block_index = touch_ends(jax.random.randint(arg_keys[3], (2, SLOTS), 0, NB), jax.random.fold_in(arg_keys[3], 1), 0, NB - 1).astype(jnp.int32)
    active_orbitals = centred(arg_keys[4], (ACT, NAO), BW ** -0.5, 0.5)
    inactive_orbitals = centred(arg_keys[5], (NIN, NAO), (NIN // 4) ** -0.5, 0.75)
    return dict(three_centre=three_centre, block_mask=block_mask, block_owner=block_owner, block_index=block_index, active_orbitals=active_orbitals, inactive_orbitals=inactive_orbitals)


def one_slot(block, row_block, col_block, living, active_split, inactive_split):
    active_rows = active_split[:, row_block, :].astype(jnp.float32)
    active_cols = active_split[:, col_block, :].astype(jnp.float32)
    half_done = jnp.einsum('pab,ub->pua', block.astype(jnp.float32), active_cols).astype(jnp.bfloat16)
    fitted = jnp.einsum('pua,ta->ptu', half_done.astype(jnp.float32), active_rows) * living
    inactive_rows = inactive_split[:, row_block, :].astype(jnp.float32)
    inactive_cols = inactive_split[:, col_block, :].astype(jnp.float32)
    density = jnp.einsum('ka,kb->ab', inactive_rows, inactive_cols).astype(jnp.bfloat16)
    coupling = jnp.einsum('pab,ab->p', block.astype(jnp.float32), density.astype(jnp.float32)) * living / BW
    return (fitted.reshape(AUX, PAIRS), coupling)

def reference(three_centre, block_mask, block_owner, block_index, active_orbitals, inactive_orbitals):
    active_split = active_orbitals.reshape(ACT, NB, BW)
    inactive_split = inactive_orbitals.reshape(NIN, NB, BW)
    living_all = block_mask.astype(jnp.float32)

    def fitted_step(carry, inputs):
        block, row_block, col_block, living = inputs
        fitted, coupling = one_slot(block, row_block, col_block, living, active_split, inactive_split)
        return ((carry[0] + fitted, carry[1] + coupling), None)
    start_values = (jnp.zeros((AUX, PAIRS), jnp.float32), jnp.zeros((AUX,), jnp.float32))
    (fitted_sum, coupling_sum), _ = lax.scan(fitted_step, start_values, (three_centre, block_index[0], block_index[1], living_all))
    fitted = fitted_sum.astype(jnp.bfloat16)
    coupling = coupling_sum.astype(jnp.bfloat16).astype(jnp.float32)

    def coulomb_of(block):
        return jnp.einsum('pab,p->ab', block.astype(jnp.float32), coupling) / math.sqrt(AUX)
    coulomb = lax.map(coulomb_of, three_centre)
    owners = jnp.arange(N_PAIR, dtype=jnp.int32)
    flagged = ((block_owner[:, None] == owners[None, :]) & (block_mask[:, None] == 1)).astype(jnp.int32)
    slot_rank = lax.optimization_barrier(jnp.sum((jnp.cumsum(flagged, axis=0) - flagged) * flagged, axis=1))
    ranks = jnp.arange(OWN, dtype=jnp.int32)
    selector = flagged.T[:, None, :].astype(jnp.float32) * (slot_rank[None, None, :] == ranks[None, :, None]).astype(jnp.float32)
    fock_blocks = jnp.einsum('okg,gab->okab', selector, coulomb, precision=lax.Precision.HIGHEST).reshape(N_PAIR * OWN, BW, BW)
    active_integrals = jnp.dot(fitted.T, fitted, preferred_element_type=jnp.float32) / AUX
    return (fock_blocks, active_integrals)
```

```python
import functools
import math

import jax
import jax.numpy as jnp
from jax import lax
from jax.experimental import pallas as pl
from jax.experimental.pallas import tpu as pltpu
from jax.sharding import PartitionSpec as P

F32 = jnp.float32
BF16 = jnp.bfloat16
NT = (((1,), (1,)), ((), ()))
TN = (((0,), (0,)), ((), ()))


def remote(src, dst, send_sem, recv_sem, axis, peer):
    return pltpu.make_async_remote_copy(
        src_ref=src,
        dst_ref=dst,
        send_sem=send_sem,
        recv_sem=recv_sem,
        device_id={axis: peer},
        device_id_type=pl.DeviceIdType.MESH,
    )


def peers_of(me, count):
    return [lax.rem(me + off, count) for off in range(1, count)]


def kernel(
    n_aux,
    n_pair,
    three_hbm,
    mask_s,
    owner_s,
    index_s,
    act_v,
    inact_hbm,
    fock_o,
    gram_o,
    t_v,
    inact_v,
    act_blocks,
    coup_acc,
    coup_all,
    coup_rows,
    half_v,
    aexp_v,
    fit_part,
    fit_all,
    fit_full,
    coul_send,
    coul_recv,
    red_all,
    fock_all,
    t_sem,
    in_sem,
    c_send,
    c_recv,
    f_send,
    f_recv,
    r_send,
    r_recv,
    g_send,
    g_recv,
    m_send,
    m_recv,
    p_send,
    p_recv,
    a_send,
    a_recv,
):
    slots, rows, width = t_v.shape[0], t_v.shape[1], t_v.shape[2]
    act = act_v.shape[0]
    act_pad = half_v.shape[1]
    pairs = act * act
    chunks, chunk_rows = coul_send.shape[0], coul_send.shape[2]
    parts = fit_part.shape[0]
    part_rows = rows // parts
    owned = fock_o.shape[0]
    gram_rows = gram_o.shape[0]
    total_aux = n_aux * rows
    me_a = lax.axis_index("aux")
    me_p = lax.axis_index("pair")
    my_part = lax.rem(me_p, parts)
    mate = me_p + 1 - 2 * my_part
    aux_peers = peers_of(me_a, n_aux)
    pair_peers = peers_of(me_p, n_pair)
    reducer = me_a < chunks

    def if_reducer(body):
        if chunks == n_aux:
            body()
        else:
            pl.when(reducer)(body)

    blocks = inact_v.shape[0]
    inact_copies = [
        pltpu.make_async_copy(
            inact_hbm.at[:, n * width : (n + 1) * width], inact_v.at[n], in_sem.at[n]
        )
        for n in range(blocks)
    ]
    for copy in inact_copies:
        copy.start()
    t_copies = [
        pltpu.make_async_copy(three_hbm.at[g], t_v.at[g], t_sem.at[g]) for g in range(slots)
    ]
    for copy in t_copies:
        copy.start()

    barrier = pltpu.get_barrier_semaphore()
    for peer in aux_peers:
        pl.semaphore_signal(
            barrier, inc=1, device_id={"aux": peer}, device_id_type=pl.DeviceIdType.MESH
        )
    for peer in pair_peers:
        pl.semaphore_signal(
            barrier, inc=1, device_id={"pair": peer}, device_id_type=pl.DeviceIdType.MESH
        )

    base = me_p * slots
    living = [mask_s[base + g] for g in range(slots)]
    row_at = [index_s[0, base + g] for g in range(slots)]
    col_at = [index_s[1, base + g] for g in range(slots)]
    for n in range(blocks):
        act_blocks[n] = act_v[:, n * width : (n + 1) * width].astype(F32)

    first = lax.broadcasted_iota(jnp.int32, (pairs, act), 0) // act
    spread = (first == lax.broadcasted_iota(jnp.int32, (pairs, act), 1)).astype(BF16)
    for g in range(slots):
        rows_g = act_blocks[row_at[g]] * living[g].astype(F32)
        aexp_v[:, g * width : (g + 1) * width] = jnp.dot(
            spread, rows_g.astype(BF16), preferred_element_type=F32
        ).astype(BF16)

    for copy in inact_copies:
        copy.wait()
    step = math.gcd(rows, 4)
    for g in range(slots):
        density = lax.dot_general(
            inact_v[row_at[g]],
            inact_v[col_at[g]],
            TN,
            preferred_element_type=F32,
        )
        density = density.astype(BF16).astype(F32) * living[g].astype(F32)
        t_copies[g].wait()

        def coupling_step(i, carry, g=g, density=density):
            for j in range(step):
                p = i * step + j
                prod = t_v[g, p].astype(F32) * density
                part = jnp.sum(prod.reshape(width // 8, 8, width), axis=0)
                if g > 0:
                    part = part + coup_acc[p]
                coup_acc[p] = part
            return carry

        lax.fori_loop(0, rows // step, coupling_step, 0)
    coup_all[me_p] = jnp.sum(coup_acc[...], axis=1)

    pl.semaphore_wait(barrier, n_aux + n_pair - 2)
    coup_copies = [
        remote(coup_all.at[me_p], coup_all.at[me_p], c_send.at[i], c_recv.at[me_p], "pair", peer)
        for i, peer in enumerate(pair_peers)
    ]
    for copy in coup_copies:
        copy.start()

    zeros = jnp.zeros((act_pad - act, width), F32)
    for g in range(slots):
        cols_g = jnp.concatenate([act_blocks[col_at[g]], zeros], axis=0).astype(BF16)

        def half_step(i, carry, g=g, cols_g=cols_g):
            block = t_v[g, pl.ds(i * step, step)].reshape(step * width, width)
            half = lax.dot_general(cols_g, block, NT, preferred_element_type=F32)
            for j in range(step):
                half_v[i * step + j, :, g * width : (g + 1) * width] = half[
                    :, j * width : (j + 1) * width
                ].astype(BF16)
            return carry

        lax.fori_loop(0, rows // step, half_step, 0)
    second = lax.rem(lax.broadcasted_iota(jnp.int32, (act_pad, pairs), 1), act)
    keep = (second == lax.broadcasted_iota(jnp.int32, (act_pad, pairs), 0)).astype(F32)
    fit_part[...] = jnp.zeros(fit_part.shape, F32)
    for h in range(parts):
        block = half_v[h * part_rows : (h + 1) * part_rows].reshape(part_rows * act_pad, -1)
        full = lax.dot_general(block, aexp_v[...], NT, preferred_element_type=F32)
        full = full.reshape(part_rows, act_pad, pairs) * keep[None]
        fit_part[h, 0:part_rows, :] = jnp.sum(full, axis=1)
    fit_copies = [
        remote(
            fit_part.at[lax.rem(peer, parts)],
            fit_all.at[me_p],
            f_send.at[i],
            f_recv.at[me_p],
            "pair",
            peer,
        )
        for i, peer in enumerate(pair_peers)
    ]
    for copy in fit_copies:
        copy.start()

    for i, peer in enumerate(pair_peers):
        remote(
            coup_all.at[peer], coup_all.at[peer], c_send.at[i], c_recv.at[peer], "pair", peer
        ).wait_recv()
    coupling = jnp.sum(jnp.sum(coup_all[...], axis=0), axis=1, keepdims=True) * (1.0 / width)
    coupling = coupling.astype(BF16).astype(F32)
    coup_rows[...] = jnp.broadcast_to(coupling, coup_rows.shape)
    for g in range(slots):

        def coulomb_step(i, total, g=g):
            for j in range(step):
                p = i * step + j
                total = total + t_v[g, p].astype(F32) * coup_rows[pl.ds(p, 1), :]
            return total

        total = lax.fori_loop(0, rows // step, coulomb_step, jnp.zeros((width, width), F32))
        coul_send[:, g] = total.astype(BF16).reshape(chunks, chunk_rows, width)

    def each_target(body):
        for off in range(chunks):
            if chunks == n_aux:
                if off > 0:
                    body(off, lax.rem(me_a + off, n_aux))
            else:
                pl.when(me_a != off)(functools.partial(body, off, off))

    def start_chunk(i, peer):
        remote(
            coul_send.at[peer], coul_recv.at[me_a], r_send.at[i], r_recv.at[me_a], "aux", peer
        ).start()

    def end_chunk(i, peer):
        remote(
            coul_send.at[peer], coul_recv.at[me_a], r_send.at[i], r_recv.at[me_a], "aux", peer
        ).wait_send()

    each_target(start_chunk)

    for i, peer in enumerate(pair_peers):
        remote(
            fit_part.at[0], fit_all.at[peer], f_send.at[i], f_recv.at[peer], "pair", peer
        ).wait_recv()
    fit_all[me_p] = fit_part[my_part]
    fit_full[my_part, me_a] = jnp.sum(fit_all[...], axis=0).astype(BF16)
    fit_gather = [
        remote(
            fit_full.at[my_part, me_a],
            fit_full.at[my_part, me_a],
            g_send.at[i],
            g_recv.at[me_a],
            "aux",
            peer,
        )
        for i, peer in enumerate(aux_peers)
    ]
    for copy in fit_gather:
        copy.start()

    def reduce_chunk():
        total = coul_send[me_a].astype(F32)
        for i, peer in enumerate(aux_peers):
            remote(
                coul_recv.at[peer], coul_recv.at[peer], r_send.at[0], r_recv.at[peer], "aux", peer
            ).wait_recv()
            total = total + coul_recv[peer].astype(F32)
        red_all[me_p] = (total * (1.0 / math.sqrt(total_aux))).astype(BF16)
        for i, peer in enumerate(pair_peers):
            remote(
                red_all.at[me_p], red_all.at[me_p], p_send.at[i], p_recv.at[me_p], "pair", peer
            ).start()

    if_reducer(reduce_chunk)

    places = []
    count = jnp.int32(0)
    for h in range(n_pair * slots):
        mine = (owner_s[h] == me_p).astype(jnp.int32) * mask_s[h]
        count = count + mine
        places.append(count * mine)

    def place_chunk():
        for i, peer in enumerate(pair_peers):
            remote(
                red_all.at[peer], red_all.at[peer], p_send.at[i], p_recv.at[peer], "pair", peer
            ).wait_recv()
        for k in range(owned):
            block = jnp.zeros((chunk_rows, width), F32)
            for h in range(k, n_pair * slots):
                weight = (places[h] == k + 1).astype(F32)
                block = block + weight * red_all[h // slots, h % slots].astype(F32)
            fock_all[me_a, k] = block.astype(BF16)
        for i, peer in enumerate(aux_peers):
            remote(
                fock_all.at[me_a], fock_all.at[me_a], a_send.at[i], a_recv.at[me_a], "aux", peer
            ).start()
        for k in range(owned):
            fock_o[k, pl.ds(pl.multiple_of(me_a * chunk_rows, chunk_rows), chunk_rows), :] = (
                fock_all[me_a, k].astype(F32)
            )

    if_reducer(place_chunk)

    for i, peer in enumerate(aux_peers):
        remote(
            fit_full.at[my_part, peer],
            fit_full.at[my_part, peer],
            g_send.at[i],
            g_recv.at[peer],
            "aux",
            peer,
        ).wait_recv()
    to_mate = remote(
        fit_full.at[my_part], fit_full.at[my_part], m_send, m_recv, "pair", mate
    )
    to_mate.start()
    remote(
        fit_full.at[1 - my_part], fit_full.at[1 - my_part], m_send, m_recv, "pair", mate
    ).wait_recv()
    fitted = fit_full[...].reshape(-1, pairs)
    picked = lax.broadcasted_iota(jnp.int32, (gram_rows, pairs), 0) + me_a * gram_rows
    pick = (picked == lax.broadcasted_iota(jnp.int32, (gram_rows, pairs), 1)).astype(BF16)
    left = lax.dot_general(pick, fitted, NT, preferred_element_type=F32).astype(BF16)
    gram_o[...] = jnp.dot(left, fitted, preferred_element_type=F32) * (1.0 / total_aux)

    def each_source(body):
        for off in range(chunks):
            if chunks == n_aux:
                if off > 0:
                    body(lax.rem(me_a + off, n_aux))
            else:
                pl.when(me_a != off)(functools.partial(body, off))

    def take_chunk(peer):
        remote(
            fock_all.at[peer], fock_all.at[peer], a_send.at[0], a_recv.at[peer], "aux", peer
        ).wait_recv()
        at = peer * chunk_rows
        if not isinstance(at, int):
            at = pl.multiple_of(at, chunk_rows)
        for k in range(owned):
            fock_o[k, pl.ds(at, chunk_rows), :] = fock_all[peer, k].astype(F32)

    each_source(take_chunk)

    for copy in coup_copies + fit_copies + fit_gather:
        copy.wait_send()
    to_mate.wait_send()
    each_target(end_chunk)

    def end_sends():
        for i, peer in enumerate(pair_peers):
            remote(
                red_all.at[me_p], red_all.at[me_p], p_send.at[i], p_recv.at[me_p], "pair", peer
            ).wait_send()
        for i, peer in enumerate(aux_peers):
            remote(
                fock_all.at[me_a], fock_all.at[me_a], a_send.at[i], a_recv.at[me_a], "aux", peer
            ).wait_send()

    if_reducer(end_sends)


def shards(three_centre, block_mask, block_owner, block_index, active_orbitals, inactive_orbitals):
    slots, rows, width, _ = three_centre.shape
    n_aux = lax.axis_size("aux")
    n_pair = lax.axis_size("pair")
    act = active_orbitals.shape[0]
    blocks = active_orbitals.shape[1] // width
    pairs = act * act
    act_pad = -(-act // 16) * 16
    chunk_rows = max(16, width // n_aux)
    chunks = width // chunk_rows
    parts = 2
    part_pad = -(-(rows // parts) // 16) * 16
    owned = n_pair * slots // 2
    dma = pltpu.SemaphoreType.DMA
    smem = pl.BlockSpec(memory_space=pltpu.SMEM)
    vmem = pl.BlockSpec(memory_space=pltpu.VMEM)
    anywhere = pl.BlockSpec(memory_space=pl.ANY)
    return pl.pallas_call(
        functools.partial(kernel, n_aux, n_pair),
        out_shape=(
            jax.ShapeDtypeStruct((owned, width, width), F32),
            jax.ShapeDtypeStruct((pairs // n_aux, pairs), F32),
        ),
        in_specs=[anywhere, smem, smem, smem, vmem, anywhere],
        out_specs=(vmem, vmem),
        scratch_shapes=[
            pltpu.VMEM(three_centre.shape, BF16),
            pltpu.VMEM((blocks, inactive_orbitals.shape[0], width), BF16),
            pltpu.VMEM((blocks, act, width), F32),
            pltpu.VMEM((rows, 8, width), F32),
            pltpu.VMEM((n_pair, rows, width), F32),
            pltpu.VMEM((rows, width), F32),
            pltpu.VMEM((rows, act_pad, slots * width), BF16),
            pltpu.VMEM((pairs, slots * width), BF16),
            pltpu.VMEM((parts, part_pad, pairs), F32),
            pltpu.VMEM((n_pair, part_pad, pairs), F32),
            pltpu.VMEM((parts, n_aux, part_pad, pairs), BF16),
            pltpu.VMEM((chunks, slots, chunk_rows, width), BF16),
            pltpu.VMEM((n_aux, slots, chunk_rows, width), BF16),
            pltpu.VMEM((n_pair, slots, chunk_rows, width), BF16),
            pltpu.VMEM((chunks, owned, chunk_rows, width), BF16),
            dma((slots,)),
            dma((blocks,)),
            dma((n_pair,)),
            dma((n_pair,)),
            dma((n_pair,)),
            dma((n_pair,)),
            dma((chunks,)),
            dma((n_aux,)),
            dma((n_aux,)),
            dma((n_aux,)),
            dma,
            dma,
            dma((n_pair,)),
            dma((n_pair,)),
            dma((n_aux,)),
            dma((chunks,)),
        ],
        compiler_params=pltpu.CompilerParams(
            collective_id=0, has_side_effects=True, vmem_limit_bytes=48 * 1024 * 1024
        ),
    )(
        three_centre,
        block_mask,
        block_owner,
        block_index,
        active_orbitals,
        inactive_orbitals,
    )


def solution(mesh):
    return jax.shard_map(
        shards,
        mesh=mesh,
        in_specs=(P("pair", "aux", None, None), P(), P(), P(), P(), P()),
        out_specs=(P("pair", None, None), P("aux", None)),
        check_vma=False,
    )
```

```python
import functools
import math

import jax
import jax.numpy as jnp
from jax import lax
from jax.experimental import pallas as pl
from jax.experimental.pallas import tpu as pltpu
from jax.sharding import PartitionSpec as P

F32 = jnp.float32
BF16 = jnp.bfloat16
NT = (((1,), (1,)), ((), ()))
TN = (((0,), (0,)), ((), ()))


def remote(src, dst, send_sem, recv_sem, axis, peer):
    return pltpu.make_async_remote_copy(
        src_ref=src,
        dst_ref=dst,
        send_sem=send_sem,
        recv_sem=recv_sem,
        device_id={axis: peer},
        device_id_type=pl.DeviceIdType.MESH,
    )


def peers_of(me, count):
    return [lax.rem(me + off, count) for off in range(1, count)]


def kernel(
    n_aux,
    n_pair,
    three_hbm,
    mask_hbm,
    owner_hbm,
    index_hbm,
    act_hbm,
    inact_hbm,
    fock_o,
    gram_o,
    mask_s,
    owner_s,
    index_s,
    act_v,
    t_v,
    inact_v,
    act_blocks,
    coup_acc,
    coup_all,
    coup_rows,
    half_v,
    aexp_v,
    fit_part,
    fit_all,
    fit_full,
    coul_send,
    coul_recv,
    red_all,
    fock_all,
    s_sem,
    t_sem,
    in_sem,
    c_send,
    c_recv,
    f_send,
    f_recv,
    r_send,
    r_recv,
    g_send,
    g_recv,
    m_send,
    m_recv,
    p_send,
    p_recv,
    a_send,
    a_recv,
):
    slots, rows, width = t_v.shape[0], t_v.shape[1], t_v.shape[2]
    act = act_v.shape[0]
    act_pad = half_v.shape[1]
    pairs = act * act
    chunks, chunk_rows = coul_send.shape[0], coul_send.shape[2]
    parts = fit_part.shape[0]
    part_rows = rows // parts
    owned = fock_o.shape[0]
    gram_rows = gram_o.shape[0]
    total_aux = n_aux * rows
    me_a = lax.axis_index("aux")
    me_p = lax.axis_index("pair")
    my_part = lax.rem(me_p, parts)
    mate = me_p + 1 - 2 * my_part
    aux_peers = peers_of(me_a, n_aux)
    pair_peers = peers_of(me_p, n_pair)
    reducer = me_a < chunks

    def if_reducer(body):
        if chunks == n_aux:
            body()
        else:
            pl.when(reducer)(body)

    small_copies = [
        pltpu.make_async_copy(source, target, s_sem.at[i])
        for i, (source, target) in enumerate(
            [(mask_hbm, mask_s), (owner_hbm, owner_s), (index_hbm, index_s), (act_hbm, act_v)]
        )
    ]
    for copy in small_copies:
        copy.start()
    blocks = inact_v.shape[0]
    inact_copies = [
        pltpu.make_async_copy(
            inact_hbm.at[:, n * width : (n + 1) * width], inact_v.at[n], in_sem.at[n]
        )
        for n in range(blocks)
    ]
    for copy in inact_copies:
        copy.start()
    t_copies = [
        pltpu.make_async_copy(three_hbm.at[g], t_v.at[g], t_sem.at[g]) for g in range(slots)
    ]
    for copy in t_copies:
        copy.start()

    barrier = pltpu.get_barrier_semaphore()
    for peer in aux_peers:
        pl.semaphore_signal(
            barrier, inc=1, device_id={"aux": peer}, device_id_type=pl.DeviceIdType.MESH
        )
    for peer in pair_peers:
        pl.semaphore_signal(
            barrier, inc=1, device_id={"pair": peer}, device_id_type=pl.DeviceIdType.MESH
        )

    for copy in small_copies:
        copy.wait()
    base = me_p * slots
    living = [mask_s[base + g] for g in range(slots)]
    row_at = [index_s[0, base + g] for g in range(slots)]
    col_at = [index_s[1, base + g] for g in range(slots)]
    for n in range(blocks):
        act_blocks[n] = act_v[:, n * width : (n + 1) * width].astype(F32)

    first = lax.broadcasted_iota(jnp.int32, (pairs, act), 0) // act
    spread = (first == lax.broadcasted_iota(jnp.int32, (pairs, act), 1)).astype(BF16)
    for g in range(slots):
        rows_g = act_blocks[row_at[g]] * living[g].astype(F32)
        aexp_v[:, g * width : (g + 1) * width] = jnp.dot(
            spread, rows_g.astype(BF16), preferred_element_type=F32
        ).astype(BF16)

    place_at = [jnp.int32(0)] * owned
    place_on = [jnp.int32(0)] * owned
    count = jnp.int32(0)
    for h in range(n_pair * slots):
        mine = (owner_s[h] == me_p).astype(jnp.int32) * mask_s[h]
        count = count + mine
        place = count * mine
        for k in range(min(owned, h + 1)):
            hit = (place == k + 1).astype(jnp.int32)
            place_at[k] = place_at[k] + hit * h
            place_on[k] = place_on[k] + hit
    place_on = [on.astype(F32) for on in place_on]

    for copy in inact_copies:
        copy.wait()
    step = math.gcd(rows, 4)
    for g in range(slots):
        density = lax.dot_general(
            inact_v[row_at[g]],
            inact_v[col_at[g]],
            TN,
            preferred_element_type=F32,
        )
        density = density.astype(BF16).astype(F32) * living[g].astype(F32)
        t_copies[g].wait()

        def coupling_step(i, carry, g=g, density=density):
            for j in range(step):
                p = i * step + j
                prod = t_v[g, p].astype(F32) * density
                part = jnp.sum(prod.reshape(width // 8, 8, width), axis=0)
                if g > 0:
                    part = part + coup_acc[p]
                coup_acc[p] = part
            return carry

        lax.fori_loop(0, rows // step, coupling_step, 0)
    coup_all[me_p] = jnp.sum(coup_acc[...], axis=1)

    pl.semaphore_wait(barrier, n_aux + n_pair - 2)
    coup_copies = [
        remote(coup_all.at[me_p], coup_all.at[me_p], c_send.at[i], c_recv.at[me_p], "pair", peer)
        for i, peer in enumerate(pair_peers)
    ]
    for copy in coup_copies:
        copy.start()

    zeros = jnp.zeros((act_pad - act, width), F32)
    for g in range(slots):
        cols_g = jnp.concatenate([act_blocks[col_at[g]], zeros], axis=0).astype(BF16)

        def half_step(i, carry, g=g, cols_g=cols_g):
            block = t_v[g, pl.ds(i * step, step)].reshape(step * width, width)
            half = lax.dot_general(cols_g, block, NT, preferred_element_type=F32)
            for j in range(step):
                half_v[i * step + j, :, g * width : (g + 1) * width] = half[
                    :, j * width : (j + 1) * width
                ].astype(BF16)
            return carry

        lax.fori_loop(0, rows // step, half_step, 0)
    for i, peer in enumerate(pair_peers):
        remote(
            coup_all.at[peer], coup_all.at[peer], c_send.at[i], c_recv.at[peer], "pair", peer
        ).wait_recv()
    coupling = jnp.sum(jnp.sum(coup_all[...], axis=0), axis=1, keepdims=True) * (1.0 / width)
    coupling = coupling.astype(BF16).astype(F32)
    coup_rows[...] = jnp.broadcast_to(coupling, coup_rows.shape)
    for g in range(slots):

        def coulomb_step(i, total, g=g):
            for j in range(step):
                p = i * step + j
                total = total + t_v[g, p].astype(F32) * coup_rows[pl.ds(p, 1), :]
            return total

        total = lax.fori_loop(0, rows // step, coulomb_step, jnp.zeros((width, width), F32))
        coul_send[:, g] = total.astype(BF16).reshape(chunks, chunk_rows, width)

    def each_target(body):
        for off in range(chunks):
            if chunks == n_aux:
                if off > 0:
                    body(off, lax.rem(me_a + off, n_aux))
            else:
                pl.when(me_a != off)(functools.partial(body, off, off))

    def start_chunk(i, peer):
        remote(
            coul_send.at[peer], coul_recv.at[me_a], r_send.at[i], r_recv.at[me_a], "aux", peer
        ).start()

    def end_chunk(i, peer):
        remote(
            coul_send.at[peer], coul_recv.at[me_a], r_send.at[i], r_recv.at[me_a], "aux", peer
        ).wait_send()

    each_target(start_chunk)

    second = lax.rem(lax.broadcasted_iota(jnp.int32, (act_pad, pairs), 1), act)
    keep = (second == lax.broadcasted_iota(jnp.int32, (act_pad, pairs), 0)).astype(F32)
    fit_part[...] = jnp.zeros(fit_part.shape, F32)
    for h in range(parts):
        block = half_v[h * part_rows : (h + 1) * part_rows].reshape(part_rows * act_pad, -1)
        full = lax.dot_general(block, aexp_v[...], NT, preferred_element_type=F32)
        full = full.reshape(part_rows, act_pad, pairs) * keep[None]
        fit_part[h, 0:part_rows, :] = jnp.sum(full, axis=1)
    fit_copies = [
        remote(
            fit_part.at[lax.rem(peer, parts)],
            fit_all.at[me_p],
            f_send.at[i],
            f_recv.at[me_p],
            "pair",
            peer,
        )
        for i, peer in enumerate(pair_peers)
    ]
    for copy in fit_copies:
        copy.start()

    def red_copy(i, peer):
        ref = red_all.at[pl.ds(me_p * slots, slots)]
        return remote(ref, ref, p_send.at[i], p_recv.at[me_p], "pair", peer)

    def reduce_chunk():
        total = coul_send[me_a].astype(F32)
        for i, peer in enumerate(aux_peers):
            remote(
                coul_recv.at[peer], coul_recv.at[peer], r_send.at[0], r_recv.at[peer], "aux", peer
            ).wait_recv()
            total = total + coul_recv[peer].astype(F32)
        red_all[pl.ds(me_p * slots, slots)] = (total * (1.0 / math.sqrt(total_aux))).astype(BF16)
        for i, peer in enumerate(pair_peers):
            red_copy(i, peer).start()

    if_reducer(reduce_chunk)

    for i, peer in enumerate(pair_peers):
        remote(
            fit_part.at[0], fit_all.at[peer], f_send.at[i], f_recv.at[peer], "pair", peer
        ).wait_recv()
    fit_all[me_p] = fit_part[my_part]
    fit_full[my_part, me_a] = jnp.sum(fit_all[...], axis=0).astype(BF16)

    neighbour = me_a + 1 - 2 * lax.rem(me_a, 2)
    evens = [lax.rem(me_a + 2 * i, n_aux) for i in range(1, n_aux // 2)]

    def fit_copy(source, peer, sem):
        ref = fit_full.at[my_part, source]
        return remote(ref, ref, g_send.at[sem], g_recv.at[source], "aux", peer)

    def fock_copy(source, peer, sem):
        return remote(
            fock_all.at[source], fock_all.at[source], a_send.at[sem], a_recv.at[source], "aux", peer
        )

    def fan_out(copy):
        for i, peer in enumerate(evens):
            copy(me_a, peer, i + 1).start()
        copy(me_a, neighbour, 0).start()

    fan_out(fit_copy)

    def place_chunk():
        for i, peer in enumerate(pair_peers):
            remote(
                red_all.at[pl.ds(peer * slots, slots)],
                red_all.at[pl.ds(peer * slots, slots)],
                p_send.at[i],
                p_recv.at[peer],
                "pair",
                peer,
            ).wait_recv()
        for k in range(owned):
            block = red_all[place_at[k]].astype(F32) * place_on[k]
            fock_all[me_a, k] = block.astype(BF16)
        fan_out(fock_copy)

    if_reducer(place_chunk)

    for i, source in enumerate(evens):
        fit_copy(source, neighbour, 0).wait_recv()
        fit_copy(source, neighbour, n_aux // 2 + i).start()

    def spread_chunk(source):
        at = pl.multiple_of(source * chunk_rows, chunk_rows)
        for k in range(owned):
            fock_o[k, pl.ds(at, chunk_rows), :] = fock_all[source, k].astype(F32)

    my_side = lax.rem(me_a, 2)
    if chunks == n_aux:
        near = [me_a] + evens
        far = [source + 1 - 2 * my_side for source in near]
    else:
        near = [2 * j + my_side for j in range(chunks // 2)]
        far = [2 * j + 1 - my_side for j in range(chunks // 2)]

    for j, source in enumerate(near):

        def pass_on(source=source, j=j):
            fock_copy(source, neighbour, 0).wait_recv()
            fock_copy(source, neighbour, n_aux // 2 + j).start()

        if chunks < n_aux:
            pl.when(me_a != source)(pass_on)
        elif j > 0:
            pass_on()

    for source in [me_a] + evens:
        fit_copy(source + 1 - 2 * my_side, neighbour, 0).wait_recv()
    to_mate = remote(fit_full.at[my_part], fit_full.at[my_part], m_send, m_recv, "pair", mate)
    to_mate.start()
    for source in near:
        spread_chunk(source)
    remote(
        fit_full.at[1 - my_part], fit_full.at[1 - my_part], m_send, m_recv, "pair", mate
    ).wait_recv()
    fitted = fit_full[...].reshape(-1, pairs)
    picked = lax.broadcasted_iota(jnp.int32, (gram_rows, pairs), 0) + me_a * gram_rows
    pick = (picked == lax.broadcasted_iota(jnp.int32, (gram_rows, pairs), 1)).astype(BF16)
    left = lax.dot_general(pick, fitted, NT, preferred_element_type=F32).astype(BF16)
    gram_o[...] = jnp.dot(left, fitted, preferred_element_type=F32) * (1.0 / total_aux)

    for source in far:
        fock_copy(source, neighbour, 0).wait_recv()
        spread_chunk(source)

    for copy in coup_copies + fit_copies:
        copy.wait_send()
    to_mate.wait_send()
    each_target(end_chunk)
    for i in range(n_aux - 1):
        fit_copy(me_a, neighbour, i).wait_send()

    def end_sends():
        for i, peer in enumerate(pair_peers):
            red_copy(i, peer).wait_send()
        for i in range(n_aux // 2):
            fock_copy(me_a, neighbour, i).wait_send()

    if_reducer(end_sends)
    for j, source in enumerate(near):

        def end_pass(source=source, j=j):
            fock_copy(source, neighbour, n_aux // 2 + j).wait_send()

        if chunks < n_aux:
            pl.when(me_a != source)(end_pass)
        elif j > 0:
            end_pass()


def shards(three_centre, block_mask, block_owner, block_index, active_orbitals, inactive_orbitals):
    slots, rows, width, _ = three_centre.shape
    n_aux = lax.axis_size("aux")
    n_pair = lax.axis_size("pair")
    act = active_orbitals.shape[0]
    blocks = active_orbitals.shape[1] // width
    pairs = act * act
    act_pad = -(-act // 16) * 16
    chunk_rows = max(16, width // n_aux)
    chunks = width // chunk_rows
    parts = 2
    part_pad = -(-(rows // parts) // 16) * 16
    owned = n_pair * slots // 2
    dma = pltpu.SemaphoreType.DMA
    vmem = pl.BlockSpec(memory_space=pltpu.VMEM)
    hbm = pl.BlockSpec(memory_space=pltpu.HBM)
    return pl.pallas_call(
        functools.partial(kernel, n_aux, n_pair),
        out_shape=(
            jax.ShapeDtypeStruct((owned, width, width), F32),
            jax.ShapeDtypeStruct((pairs // n_aux, pairs), F32),
        ),
        in_specs=[hbm] * 6,
        out_specs=(vmem, vmem),
        scratch_shapes=[
            pltpu.SMEM(block_mask.shape, jnp.int32),
            pltpu.SMEM(block_owner.shape, jnp.int32),
            pltpu.SMEM(block_index.shape, jnp.int32),
            pltpu.VMEM(active_orbitals.shape, BF16),
            pltpu.VMEM(three_centre.shape, BF16),
            pltpu.VMEM((blocks, inactive_orbitals.shape[0], width), BF16),
            pltpu.VMEM((blocks, act, width), F32),
            pltpu.VMEM((rows, 8, width), F32),
            pltpu.VMEM((n_pair, rows, width), F32),
            pltpu.VMEM((rows, width), F32),
            pltpu.VMEM((rows, act_pad, slots * width), BF16),
            pltpu.VMEM((pairs, slots * width), BF16),
            pltpu.VMEM((parts, part_pad, pairs), F32),
            pltpu.VMEM((n_pair, part_pad, pairs), F32),
            pltpu.VMEM((parts, n_aux, part_pad, pairs), BF16),
            pltpu.VMEM((chunks, slots, chunk_rows, width), BF16),
            pltpu.VMEM((n_aux, slots, chunk_rows, width), BF16),
            pltpu.VMEM((n_pair * slots, chunk_rows, width), BF16),
            pltpu.VMEM((chunks, owned, chunk_rows, width), BF16),
            dma((4,)),
            dma((slots,)),
            dma((blocks,)),
            dma((n_pair,)),
            dma((n_pair,)),
            dma((n_pair,)),
            dma((n_pair,)),
            dma((chunks,)),
            dma((n_aux,)),
            dma((n_aux,)),
            dma((n_aux,)),
            dma,
            dma,
            dma((n_pair,)),
            dma((n_pair,)),
            dma((n_aux,)),
            dma((chunks,)),
        ],
        compiler_params=pltpu.CompilerParams(
            collective_id=0, has_side_effects=True, vmem_limit_bytes=60 * 1024 * 1024
        ),
    )(
        three_centre,
        block_mask,
        block_owner,
        block_index,
        active_orbitals,
        inactive_orbitals,
    )


def solution(mesh):
    return jax.shard_map(
        shards,
        mesh=mesh,
        in_specs=(P("pair", "aux", None, None), P(), P(), P(), P(), P()),
        out_specs=(P("pair", None, None), P("aux", None)),
        check_vma=False,
    )
```

```python
import functools
import math

import jax
import jax.numpy as jnp
from jax import lax
from jax.experimental import pallas as pl
from jax.experimental.pallas import tpu as pltpu
from jax.sharding import PartitionSpec as P

F32 = jnp.float32
BF16 = jnp.bfloat16
NT = (((1,), (1,)), ((), ()))
TN = (((0,), (0,)), ((), ()))


def remote(src, dst, send_sem, recv_sem, axis, peer):
    return pltpu.make_async_remote_copy(
        src_ref=src,
        dst_ref=dst,
        send_sem=send_sem,
        recv_sem=recv_sem,
        device_id={axis: peer},
        device_id_type=pl.DeviceIdType.MESH,
    )


def peers_of(me, count):
    return [lax.rem(me + off, count) for off in range(1, count)]


def kernel(
    n_aux,
    n_pair,
    three_hbm,
    mask_hbm,
    owner_hbm,
    index_hbm,
    act_hbm,
    inact_hbm,
    fock_o,
    gram_o,
    mask_s,
    owner_s,
    index_s,
    act_v,
    t_v,
    inact_v,
    act_blocks,
    coup_acc,
    coup_all,
    coup_rows,
    half_v,
    aexp_v,
    fit_part,
    fit_all,
    fit_full,
    coul_send,
    coul_recv,
    red_all,
    fock_all,
    s_sem,
    t_sem,
    in_sem,
    c_send,
    c_recv,
    f_send,
    f_recv,
    r_send,
    r_recv,
    g_send,
    g_recv,
    m_send,
    m_recv,
    p_send,
    p_recv,
    a_send,
    a_recv,
):
    slots, rows, width = t_v.shape[0], t_v.shape[1], t_v.shape[2]
    act = act_v.shape[0]
    act_pad = half_v.shape[1]
    pairs = act * act
    chunks, chunk_rows = coul_send.shape[0], coul_send.shape[2]
    parts = fit_part.shape[0]
    part_rows = rows // parts
    owned = fock_o.shape[0]
    gram_rows = gram_o.shape[0]
    total_aux = n_aux * rows
    me_a = lax.axis_index("aux")
    me_p = lax.axis_index("pair")
    my_part = lax.rem(me_p, parts)
    mate = me_p + 1 - 2 * my_part
    aux_peers = peers_of(me_a, n_aux)
    pair_peers = peers_of(me_p, n_pair)
    reducer = me_a < chunks

    def if_reducer(body):
        if chunks == n_aux:
            body()
        else:
            pl.when(reducer)(body)

    small_copies = [
        pltpu.make_async_copy(source, target, s_sem.at[i])
        for i, (source, target) in enumerate(
            [(mask_hbm, mask_s), (owner_hbm, owner_s), (index_hbm, index_s), (act_hbm, act_v)]
        )
    ]
    for copy in small_copies:
        copy.start()
    blocks = inact_v.shape[0]
    inact_copies = [
        pltpu.make_async_copy(
            inact_hbm.at[:, n * width : (n + 1) * width], inact_v.at[n], in_sem.at[n]
        )
        for n in range(blocks)
    ]
    for copy in inact_copies:
        copy.start()
    t_copies = [
        pltpu.make_async_copy(three_hbm.at[g], t_v.at[g], t_sem.at[g]) for g in range(slots)
    ]
    for copy in t_copies:
        copy.start()

    barrier = pltpu.get_barrier_semaphore()
    for peer in aux_peers:
        pl.semaphore_signal(
            barrier, inc=1, device_id={"aux": peer}, device_id_type=pl.DeviceIdType.MESH
        )
    for peer in pair_peers:
        pl.semaphore_signal(
            barrier, inc=1, device_id={"pair": peer}, device_id_type=pl.DeviceIdType.MESH
        )

    for copy in small_copies:
        copy.wait()
    base = me_p * slots
    living = [mask_s[base + g] for g in range(slots)]
    row_at = [index_s[0, base + g] for g in range(slots)]
    col_at = [index_s[1, base + g] for g in range(slots)]
    for n in range(blocks):
        act_blocks[n] = act_v[:, n * width : (n + 1) * width].astype(F32)

    first = lax.broadcasted_iota(jnp.int32, (pairs, act), 0) // act
    spread = (first == lax.broadcasted_iota(jnp.int32, (pairs, act), 1)).astype(BF16)
    for g in range(slots):
        rows_g = act_blocks[row_at[g]] * living[g].astype(F32)
        aexp_v[:, g * width : (g + 1) * width] = jnp.dot(
            spread, rows_g.astype(BF16), preferred_element_type=F32
        ).astype(BF16)

    place_at = [jnp.int32(0)] * owned
    place_on = [jnp.int32(0)] * owned
    count = jnp.int32(0)
    for h in range(n_pair * slots):
        mine = (owner_s[h] == me_p).astype(jnp.int32) * mask_s[h]
        count = count + mine
        place = count * mine
        for k in range(min(owned, h + 1)):
            hit = (place == k + 1).astype(jnp.int32)
            place_at[k] = place_at[k] + hit * h
            place_on[k] = place_on[k] + hit
    place_on = [on.astype(F32) for on in place_on]

    for copy in inact_copies:
        copy.wait()
    step = math.gcd(rows, 4)
    for g in range(slots):
        density = lax.dot_general(
            inact_v[row_at[g]],
            inact_v[col_at[g]],
            TN,
            preferred_element_type=F32,
        )
        density = density.astype(BF16).astype(F32) * living[g].astype(F32)
        t_copies[g].wait()

        def coupling_step(i, carry, g=g, density=density):
            for j in range(step):
                p = i * step + j
                prod = t_v[g, p].astype(F32) * density
                part = jnp.sum(prod.reshape(width // 8, 8, width), axis=0)
                if g > 0:
                    part = part + coup_acc[p]
                coup_acc[p] = part
            return carry

        lax.fori_loop(0, rows // step, coupling_step, 0)
    coup_all[me_p] = jnp.sum(coup_acc[...], axis=1)

    pl.semaphore_wait(barrier, n_aux + n_pair - 2)
    coup_copies = [
        remote(coup_all.at[me_p], coup_all.at[me_p], c_send.at[i], c_recv.at[me_p], "pair", peer)
        for i, peer in enumerate(pair_peers)
    ]
    for copy in coup_copies:
        copy.start()

    zeros = jnp.zeros((act_pad - act, width), F32)
    for g in range(slots):
        cols_g = jnp.concatenate([act_blocks[col_at[g]], zeros], axis=0).astype(BF16)

        def half_step(i, carry, g=g, cols_g=cols_g):
            block = t_v[g, pl.ds(i * step, step)].reshape(step * width, width)
            half = lax.dot_general(cols_g, block, NT, preferred_element_type=F32)
            for j in range(step):
                half_v[i * step + j, :, g * width : (g + 1) * width] = half[
                    :, j * width : (j + 1) * width
                ].astype(BF16)
            return carry

        lax.fori_loop(0, rows // step, half_step, 0)
    for i, peer in enumerate(pair_peers):
        remote(
            coup_all.at[peer], coup_all.at[peer], c_send.at[i], c_recv.at[peer], "pair", peer
        ).wait_recv()
    coupling = jnp.sum(jnp.sum(coup_all[...], axis=0), axis=1, keepdims=True) * (1.0 / width)
    coupling = coupling.astype(BF16).astype(F32)
    coup_rows[...] = jnp.broadcast_to(coupling, coup_rows.shape)
    def each_target(body):
        for off in range(chunks):
            if chunks == n_aux:
                if off > 0:
                    body(off, lax.rem(me_a + off, n_aux))
            else:
                pl.when(me_a != off)(functools.partial(body, off, off))

    def chunk_copy(g, i, peer):
        return remote(
            coul_send.at[peer, g],
            coul_recv.at[me_a, g],
            r_send.at[g, i],
            r_recv.at[g, me_a],
            "aux",
            peer,
        )

    def start_chunk(g, i, peer):
        chunk_copy(g, i, peer).start()

    def end_chunk(g, i, peer):
        chunk_copy(g, i, peer).wait_send()

    for g in range(slots):

        def coulomb_step(i, total, g=g):
            for j in range(step):
                p = i * step + j
                total = total + t_v[g, p].astype(F32) * coup_rows[pl.ds(p, 1), :]
            return total

        total = lax.fori_loop(0, rows // step, coulomb_step, jnp.zeros((width, width), F32))
        coul_send[:, g] = total.astype(BF16).reshape(chunks, chunk_rows, width)
        each_target(functools.partial(start_chunk, g))

    second = lax.rem(lax.broadcasted_iota(jnp.int32, (act_pad, pairs), 1), act)
    keep = (second == lax.broadcasted_iota(jnp.int32, (act_pad, pairs), 0)).astype(F32)
    fit_part[...] = jnp.zeros(fit_part.shape, F32)
    for h in range(parts):
        block = half_v[h * part_rows : (h + 1) * part_rows].reshape(part_rows * act_pad, -1)
        full = lax.dot_general(block, aexp_v[...], NT, preferred_element_type=F32)
        full = full.reshape(part_rows, act_pad, pairs) * keep[None]
        fit_part[h, 0:part_rows, :] = jnp.sum(full, axis=1)
    fit_copies = [
        remote(
            fit_part.at[lax.rem(peer, parts)],
            fit_all.at[me_p],
            f_send.at[i],
            f_recv.at[me_p],
            "pair",
            peer,
        )
        for i, peer in enumerate(pair_peers)
    ]
    for copy in fit_copies:
        copy.start()

    def red_copy(i, peer):
        ref = red_all.at[pl.ds(me_p * slots, slots)]
        return remote(ref, ref, p_send.at[i], p_recv.at[me_p], "pair", peer)

    def reduce_chunk():
        for g in range(slots):
            total = coul_send[me_a, g].astype(F32)
            for peer in aux_peers:
                ref = coul_recv.at[peer, g]
                remote(ref, ref, r_send.at[0, 0], r_recv.at[g, peer], "aux", peer).wait_recv()
                total = total + coul_recv[peer, g].astype(F32)
            red_all[me_p * slots + g] = (total * (1.0 / math.sqrt(total_aux))).astype(BF16)
        for i, peer in enumerate(pair_peers):
            red_copy(i, peer).start()

    if_reducer(reduce_chunk)

    for i, peer in enumerate(pair_peers):
        remote(
            fit_part.at[0], fit_all.at[peer], f_send.at[i], f_recv.at[peer], "pair", peer
        ).wait_recv()
    fit_all[me_p] = fit_part[my_part]
    fit_full[my_part, me_a] = jnp.sum(fit_all[...], axis=0).astype(BF16)

    neighbour = me_a + 1 - 2 * lax.rem(me_a, 2)
    evens = [lax.rem(me_a + 2 * i, n_aux) for i in range(1, n_aux // 2)]

    def fit_copy(source, peer, sem):
        ref = fit_full.at[my_part, source]
        return remote(ref, ref, g_send.at[sem], g_recv.at[source], "aux", peer)

    def fock_copy(source, peer, sem):
        return remote(
            fock_all.at[source], fock_all.at[source], a_send.at[sem], a_recv.at[source], "aux", peer
        )

    def fan_out(copy):
        for i, peer in enumerate(evens):
            copy(me_a, peer, i + 1).start()
        copy(me_a, neighbour, 0).start()

    fan_out(fit_copy)

    def place_chunk():
        for i, peer in enumerate(pair_peers):
            remote(
                red_all.at[pl.ds(peer * slots, slots)],
                red_all.at[pl.ds(peer * slots, slots)],
                p_send.at[i],
                p_recv.at[peer],
                "pair",
                peer,
            ).wait_recv()
        for k in range(owned):
            block = red_all[place_at[k]].astype(F32) * place_on[k]
            fock_all[me_a, k] = block.astype(BF16)
        fan_out(fock_copy)

    if_reducer(place_chunk)

    for i, source in enumerate(evens):
        fit_copy(source, neighbour, 0).wait_recv()
        fit_copy(source, neighbour, n_aux // 2 + i).start()

    def spread_chunk(source):
        at = pl.multiple_of(source * chunk_rows, chunk_rows)
        for k in range(owned):
            fock_o[k, pl.ds(at, chunk_rows), :] = fock_all[source, k].astype(F32)

    my_side = lax.rem(me_a, 2)
    if chunks == n_aux:
        near = [me_a] + evens
        far = [source + 1 - 2 * my_side for source in near]
    else:
        near = [2 * j + my_side for j in range(chunks // 2)]
        far = [2 * j + 1 - my_side for j in range(chunks // 2)]

    for j, source in enumerate(near):

        def pass_on(source=source, j=j):
            fock_copy(source, neighbour, 0).wait_recv()
            fock_copy(source, neighbour, n_aux // 2 + j).start()

        if chunks < n_aux:
            pl.when(me_a != source)(pass_on)
        elif j > 0:
            pass_on()

    for source in [me_a] + evens:
        fit_copy(source + 1 - 2 * my_side, neighbour, 0).wait_recv()
    to_mate = remote(fit_full.at[my_part], fit_full.at[my_part], m_send, m_recv, "pair", mate)
    to_mate.start()
    for source in near:
        spread_chunk(source)
    remote(
        fit_full.at[1 - my_part], fit_full.at[1 - my_part], m_send, m_recv, "pair", mate
    ).wait_recv()
    fitted = fit_full[...].reshape(-1, pairs)
    picked = lax.broadcasted_iota(jnp.int32, (gram_rows, pairs), 0) + me_a * gram_rows
    pick = (picked == lax.broadcasted_iota(jnp.int32, (gram_rows, pairs), 1)).astype(BF16)
    left = lax.dot_general(pick, fitted, NT, preferred_element_type=F32).astype(BF16)
    gram_o[...] = jnp.dot(left, fitted, preferred_element_type=F32) * (1.0 / total_aux)

    for source in far:
        fock_copy(source, neighbour, 0).wait_recv()
        spread_chunk(source)

    for copy in coup_copies + fit_copies:
        copy.wait_send()
    to_mate.wait_send()
    for g in range(slots):
        each_target(functools.partial(end_chunk, g))
    for i in range(n_aux - 1):
        fit_copy(me_a, neighbour, i).wait_send()

    def end_sends():
        for i, peer in enumerate(pair_peers):
            red_copy(i, peer).wait_send()
        for i in range(n_aux // 2):
            fock_copy(me_a, neighbour, i).wait_send()

    if_reducer(end_sends)
    for j, source in enumerate(near):

        def end_pass(source=source, j=j):
            fock_copy(source, neighbour, n_aux // 2 + j).wait_send()

        if chunks < n_aux:
            pl.when(me_a != source)(end_pass)
        elif j > 0:
            end_pass()


def finish(fock_in, gram_in, fock_out, gram_out, sem):
    owned = fock_in.shape[0]
    copies = [
        pltpu.make_async_copy(fock_in.at[k], fock_out.at[k], sem.at[k]) for k in range(owned)
    ]
    copies.append(pltpu.make_async_copy(gram_in, gram_out, sem.at[owned]))
    for copy in copies:
        copy.start()
    for copy in copies:
        copy.wait()


def shards(three_centre, block_mask, block_owner, block_index, active_orbitals, inactive_orbitals):
    slots, rows, width, _ = three_centre.shape
    n_aux = lax.axis_size("aux")
    n_pair = lax.axis_size("pair")
    act = active_orbitals.shape[0]
    blocks = active_orbitals.shape[1] // width
    pairs = act * act
    act_pad = -(-act // 16) * 16
    chunk_rows = max(16, width // n_aux)
    chunks = width // chunk_rows
    parts = 2
    part_pad = -(-(rows // parts) // 16) * 16
    owned = n_pair * slots // 2
    dma = pltpu.SemaphoreType.DMA
    vmem = pl.BlockSpec(memory_space=pltpu.VMEM)
    hbm = pl.BlockSpec(memory_space=pltpu.HBM)
    fock, gram = pl.pallas_call(
        functools.partial(kernel, n_aux, n_pair),
        out_shape=(
            jax.ShapeDtypeStruct((owned, width, width), F32),
            jax.ShapeDtypeStruct((pairs // n_aux, pairs), F32),
        ),
        in_specs=[hbm] * 6,
        out_specs=(vmem, vmem),
        scratch_shapes=[
            pltpu.SMEM(block_mask.shape, jnp.int32),
            pltpu.SMEM(block_owner.shape, jnp.int32),
            pltpu.SMEM(block_index.shape, jnp.int32),
            pltpu.VMEM(active_orbitals.shape, BF16),
            pltpu.VMEM(three_centre.shape, BF16),
            pltpu.VMEM((blocks, inactive_orbitals.shape[0], width), BF16),
            pltpu.VMEM((blocks, act, width), F32),
            pltpu.VMEM((rows, 8, width), F32),
            pltpu.VMEM((n_pair, rows, width), F32),
            pltpu.VMEM((rows, width), F32),
            pltpu.VMEM((rows, act_pad, slots * width), BF16),
            pltpu.VMEM((pairs, slots * width), BF16),
            pltpu.VMEM((parts, part_pad, pairs), F32),
            pltpu.VMEM((n_pair, part_pad, pairs), F32),
            pltpu.VMEM((parts, n_aux, part_pad, pairs), BF16),
            pltpu.VMEM((chunks, slots, chunk_rows, width), BF16),
            pltpu.VMEM((n_aux, slots, chunk_rows, width), BF16),
            pltpu.VMEM((n_pair * slots, chunk_rows, width), BF16),
            pltpu.VMEM((chunks, owned, chunk_rows, width), BF16),
            dma((4,)),
            dma((slots,)),
            dma((blocks,)),
            dma((n_pair,)),
            dma((n_pair,)),
            dma((n_pair,)),
            dma((n_pair,)),
            dma((slots, chunks)),
            dma((slots, n_aux)),
            dma((n_aux,)),
            dma((n_aux,)),
            dma,
            dma,
            dma((n_pair,)),
            dma((n_pair,)),
            dma((n_aux,)),
            dma((chunks,)),
        ],
        compiler_params=pltpu.CompilerParams(
            collective_id=0, has_side_effects=True, vmem_limit_bytes=60 * 1024 * 1024
        ),
    )(
        three_centre,
        block_mask,
        block_owner,
        block_index,
        active_orbitals,
        inactive_orbitals,
    )
    return pl.pallas_call(
        finish,
        out_shape=(
            jax.ShapeDtypeStruct(fock.shape, F32),
            jax.ShapeDtypeStruct(gram.shape, F32),
        ),
        in_specs=[hbm, hbm],
        out_specs=(hbm, hbm),
        scratch_shapes=[dma((owned + 1,))],
        compiler_params=pltpu.CompilerParams(vmem_limit_bytes=60 * 1024 * 1024),
    )(fock, gram)


def solution(mesh):
    return jax.shard_map(
        shards,
        mesh=mesh,
        in_specs=(P("pair", "aux", None, None), P(), P(), P(), P(), P()),
        out_specs=(P("pair", None, None), P("aux", None)),
        check_vma=False,
    )
```

```python
import functools
import math

import jax
import jax.numpy as jnp
from jax import lax
from jax.experimental import pallas as pl
from jax.experimental.pallas import tpu as pltpu
from jax.sharding import PartitionSpec as P

F32 = jnp.float32
BF16 = jnp.bfloat16
NT = (((1,), (1,)), ((), ()))
TN = (((0,), (0,)), ((), ()))


def remote(src, dst, send_sem, recv_sem, axis, peer):
    return pltpu.make_async_remote_copy(
        src_ref=src,
        dst_ref=dst,
        send_sem=send_sem,
        recv_sem=recv_sem,
        device_id={axis: peer},
        device_id_type=pl.DeviceIdType.MESH,
    )


def peers_of(me, count):
    return [lax.rem(me + off, count) for off in range(1, count)]


def kernel(
    n_aux,
    n_pair,
    three_hbm,
    mask_hbm,
    owner_hbm,
    index_hbm,
    act_hbm,
    inact_hbm,
    fock_o,
    gram_o,
    mask_s,
    owner_s,
    index_s,
    act_v,
    t_v,
    inact_v,
    act_blocks,
    coup_acc,
    coup_all,
    coup_rows,
    half_v,
    aexp_v,
    fit_part,
    fit_all,
    fit_full,
    coul_send,
    coul_recv,
    red_all,
    fock_all,
    s_sem,
    t_sem,
    in_sem,
    c_send,
    c_recv,
    f_send,
    f_recv,
    r_send,
    r_recv,
    g_send,
    g_recv,
    m_send,
    m_recv,
    p_send,
    p_recv,
    a_send,
    a_recv,
):
    slots, rows, width = t_v.shape[0], t_v.shape[1], t_v.shape[2]
    act = act_v.shape[0]
    act_pad = half_v.shape[1]
    pairs = act * act
    chunks, chunk_rows = coul_send.shape[0], coul_send.shape[2]
    parts = fit_part.shape[0]
    part_rows = rows // parts
    owned = fock_o.shape[0]
    gram_rows = gram_o.shape[0]
    total_aux = n_aux * rows
    me_a = lax.axis_index("aux")
    me_p = lax.axis_index("pair")
    my_part = lax.rem(me_p, parts)
    mate = me_p + 1 - 2 * my_part
    aux_peers = peers_of(me_a, n_aux)
    pair_peers = peers_of(me_p, n_pair)
    reducer = me_a < chunks

    def if_reducer(body):
        if chunks == n_aux:
            body()
        else:
            pl.when(reducer)(body)

    small_copies = [
        pltpu.make_async_copy(source, target, s_sem.at[i])
        for i, (source, target) in enumerate(
            [(mask_hbm, mask_s), (owner_hbm, owner_s), (index_hbm, index_s), (act_hbm, act_v)]
        )
    ]
    for copy in small_copies:
        copy.start()
    blocks = inact_v.shape[0]
    inact_copies = [
        pltpu.make_async_copy(
            inact_hbm.at[:, n * width : (n + 1) * width], inact_v.at[n], in_sem.at[n]
        )
        for n in range(blocks)
    ]
    for copy in inact_copies:
        copy.start()
    t_copies = [
        pltpu.make_async_copy(three_hbm.at[g], t_v.at[g], t_sem.at[g]) for g in range(slots)
    ]
    for copy in t_copies:
        copy.start()

    barrier = pltpu.get_barrier_semaphore()
    for peer in aux_peers:
        pl.semaphore_signal(
            barrier, inc=1, device_id={"aux": peer}, device_id_type=pl.DeviceIdType.MESH
        )
    for peer in pair_peers:
        pl.semaphore_signal(
            barrier, inc=1, device_id={"pair": peer}, device_id_type=pl.DeviceIdType.MESH
        )

    for copy in small_copies:
        copy.wait()
    base = me_p * slots
    living = [mask_s[base + g] for g in range(slots)]
    row_at = [index_s[0, base + g] for g in range(slots)]
    col_at = [index_s[1, base + g] for g in range(slots)]
    for n in range(blocks):
        act_blocks[n] = act_v[:, n * width : (n + 1) * width].astype(F32)

    first = lax.broadcasted_iota(jnp.int32, (pairs, act), 0) // act
    spread = (first == lax.broadcasted_iota(jnp.int32, (pairs, act), 1)).astype(BF16)
    for g in range(slots):
        rows_g = act_blocks[row_at[g]] * living[g].astype(F32)
        aexp_v[:, g * width : (g + 1) * width] = jnp.dot(
            spread, rows_g.astype(BF16), preferred_element_type=F32
        ).astype(BF16)

    place_at = [jnp.int32(0)] * owned
    place_on = [jnp.int32(0)] * owned
    count = jnp.int32(0)
    for h in range(n_pair * slots):
        mine = (owner_s[h] == me_p).astype(jnp.int32) * mask_s[h]
        count = count + mine
        place = count * mine
        for k in range(min(owned, h + 1)):
            hit = (place == k + 1).astype(jnp.int32)
            place_at[k] = place_at[k] + hit * h
            place_on[k] = place_on[k] + hit
    place_on = [on.astype(F32) for on in place_on]

    for copy in inact_copies:
        copy.wait()
    step = math.gcd(rows, 4)
    for g in range(slots):
        density = lax.dot_general(
            inact_v[row_at[g]],
            inact_v[col_at[g]],
            TN,
            preferred_element_type=F32,
        )
        density = density.astype(BF16).astype(F32) * living[g].astype(F32)
        t_copies[g].wait()

        def coupling_step(i, carry, g=g, density=density):
            for j in range(step):
                p = i * step + j
                prod = t_v[g, p].astype(F32) * density
                part = jnp.sum(prod.reshape(width // 8, 8, width), axis=0)
                if g > 0:
                    part = part + coup_acc[p]
                coup_acc[p] = part
            return carry

        lax.fori_loop(0, rows // step, coupling_step, 0)
    coup_all[me_p] = jnp.sum(coup_acc[...], axis=1)

    pl.semaphore_wait(barrier, n_aux + n_pair - 2)
    coup_copies = [
        remote(coup_all.at[me_p], coup_all.at[me_p], c_send.at[i], c_recv.at[me_p], "pair", peer)
        for i, peer in enumerate(pair_peers)
    ]
    for copy in coup_copies:
        copy.start()

    zeros = jnp.zeros((act_pad - act, width), F32)
    for g in range(slots):
        cols_g = jnp.concatenate([act_blocks[col_at[g]], zeros], axis=0).astype(BF16)

        def half_step(i, carry, g=g, cols_g=cols_g):
            block = t_v[g, pl.ds(i * step, step)].reshape(step * width, width)
            half = lax.dot_general(cols_g, block, NT, preferred_element_type=F32)
            for j in range(step):
                half_v[i * step + j, :, g * width : (g + 1) * width] = half[
                    :, j * width : (j + 1) * width
                ].astype(BF16)
            return carry

        lax.fori_loop(0, rows // step, half_step, 0)
    for i, peer in enumerate(pair_peers):
        remote(
            coup_all.at[peer], coup_all.at[peer], c_send.at[i], c_recv.at[peer], "pair", peer
        ).wait_recv()
    coupling = jnp.sum(jnp.sum(coup_all[...], axis=0), axis=1, keepdims=True) * (1.0 / width)
    coupling = coupling.astype(BF16).astype(F32)
    coup_rows[...] = jnp.broadcast_to(coupling, coup_rows.shape)
    def each_target(body):
        for off in range(chunks):
            if chunks == n_aux:
                if off > 0:
                    body(off, lax.rem(me_a + off, n_aux))
            else:
                pl.when(me_a != off)(functools.partial(body, off, off))

    def chunk_copy(g, i, peer):
        return remote(
            coul_send.at[peer, g],
            coul_recv.at[me_a, g],
            r_send.at[g, i],
            r_recv.at[g, me_a],
            "aux",
            peer,
        )

    def start_chunk(g, i, peer):
        chunk_copy(g, i, peer).start()

    def end_chunk(g, i, peer):
        chunk_copy(g, i, peer).wait_send()

    for g in range(slots):

        def coulomb_step(i, total, g=g):
            for j in range(step):
                p = i * step + j
                total = total + t_v[g, p].astype(F32) * coup_rows[pl.ds(p, 1), :]
            return total

        total = lax.fori_loop(0, rows // step, coulomb_step, jnp.zeros((width, width), F32))
        coul_send[:, g] = total.astype(BF16).reshape(chunks, chunk_rows, width)
        each_target(functools.partial(start_chunk, g))

    second = lax.rem(lax.broadcasted_iota(jnp.int32, (act_pad, pairs), 1), act)
    keep = (second == lax.broadcasted_iota(jnp.int32, (act_pad, pairs), 0)).astype(F32)
    fit_part[...] = jnp.zeros(fit_part.shape, F32)
    for h in range(parts):
        block = half_v[h * part_rows : (h + 1) * part_rows].reshape(part_rows * act_pad, -1)
        full = lax.dot_general(block, aexp_v[...], NT, preferred_element_type=F32)
        full = full.reshape(part_rows, act_pad, pairs) * keep[None]
        fit_part[h, 0:part_rows, :] = jnp.sum(full, axis=1)
    fit_copies = [
        remote(
            fit_part.at[lax.rem(peer, parts)],
            fit_all.at[me_p],
            f_send.at[i],
            f_recv.at[me_p],
            "pair",
            peer,
        )
        for i, peer in enumerate(pair_peers)
    ]
    for copy in fit_copies:
        copy.start()

    def red_copy(i, peer):
        ref = red_all.at[pl.ds(me_p * slots, slots)]
        return remote(ref, ref, p_send.at[i], p_recv.at[me_p], "pair", peer)

    def reduce_chunk():
        for g in range(slots):
            total = coul_send[me_a, g].astype(F32)
            for peer in aux_peers:
                ref = coul_recv.at[peer, g]
                remote(ref, ref, r_send.at[0, 0], r_recv.at[g, peer], "aux", peer).wait_recv()
                total = total + coul_recv[peer, g].astype(F32)
            red_all[me_p * slots + g] = (total * (1.0 / math.sqrt(total_aux))).astype(BF16)
        for i, peer in enumerate(pair_peers):
            red_copy(i, peer).start()

    if_reducer(reduce_chunk)

    for i, peer in enumerate(pair_peers):
        remote(
            fit_part.at[0], fit_all.at[peer], f_send.at[i], f_recv.at[peer], "pair", peer
        ).wait_recv()
    fit_all[me_p] = fit_part[my_part]
    fit_full[my_part, me_a] = jnp.sum(fit_all[...], axis=0).astype(BF16)

    neighbour = me_a + 1 - 2 * lax.rem(me_a, 2)
    evens = [lax.rem(me_a + 2 * i, n_aux) for i in range(1, n_aux // 2)]

    def fit_copy(source, peer, sem):
        ref = fit_full.at[my_part, source]
        return remote(ref, ref, g_send.at[sem], g_recv.at[source], "aux", peer)

    def fock_copy(source, peer, sem):
        return remote(
            fock_all.at[source], fock_all.at[source], a_send.at[sem], a_recv.at[source], "aux", peer
        )

    def fan_out(copy):
        for i, peer in enumerate(evens):
            copy(me_a, peer, i + 1).start()
        copy(me_a, neighbour, 0).start()

    fan_out(fit_copy)

    def place_chunk():
        for i, peer in enumerate(pair_peers):
            remote(
                red_all.at[pl.ds(peer * slots, slots)],
                red_all.at[pl.ds(peer * slots, slots)],
                p_send.at[i],
                p_recv.at[peer],
                "pair",
                peer,
            ).wait_recv()
        for k in range(owned):
            block = red_all[place_at[k]].astype(F32) * place_on[k]
            fock_all[me_a, k] = block.astype(BF16)
        fan_out(fock_copy)

    if_reducer(place_chunk)

    for i, source in enumerate(evens):
        fit_copy(source, neighbour, 0).wait_recv()
        fit_copy(source, neighbour, n_aux // 2 + i).start()

    def spread_chunk(source):
        at = pl.multiple_of(source * chunk_rows, chunk_rows)
        for k in range(owned):
            fock_o[k, pl.ds(at, chunk_rows), :] = fock_all[source, k].astype(F32)

    my_side = lax.rem(me_a, 2)
    if chunks == n_aux:
        near = [me_a] + evens
        far = [source + 1 - 2 * my_side for source in near]
    else:
        near = [2 * j + my_side for j in range(chunks // 2)]
        far = [2 * j + 1 - my_side for j in range(chunks // 2)]

    for j, source in enumerate(near):

        def pass_on(source=source, j=j):
            fock_copy(source, neighbour, 0).wait_recv()
            fock_copy(source, neighbour, n_aux // 2 + j).start()

        if chunks < n_aux:
            pl.when(me_a != source)(pass_on)
        elif j > 0:
            pass_on()

    for source in [me_a] + evens:
        fit_copy(source + 1 - 2 * my_side, neighbour, 0).wait_recv()
    to_mate = remote(fit_full.at[my_part], fit_full.at[my_part], m_send, m_recv, "pair", mate)
    to_mate.start()
    for source in near:
        spread_chunk(source)
    remote(
        fit_full.at[1 - my_part], fit_full.at[1 - my_part], m_send, m_recv, "pair", mate
    ).wait_recv()
    fitted = fit_full[...].reshape(-1, pairs)
    picked = lax.broadcasted_iota(jnp.int32, (gram_rows, pairs), 0) + me_a * gram_rows
    pick = (picked == lax.broadcasted_iota(jnp.int32, (gram_rows, pairs), 1)).astype(BF16)
    left = lax.dot_general(pick, fitted, NT, preferred_element_type=F32).astype(BF16)
    gram_o[...] = jnp.dot(left, fitted, preferred_element_type=F32) * (1.0 / total_aux)

    for source in far:
        fock_copy(source, neighbour, 0).wait_recv()
        spread_chunk(source)

    for copy in coup_copies + fit_copies:
        copy.wait_send()
    to_mate.wait_send()
    for g in range(slots):
        each_target(functools.partial(end_chunk, g))
    for i in range(n_aux - 1):
        fit_copy(me_a, neighbour, i).wait_send()

    def end_sends():
        for i, peer in enumerate(pair_peers):
            red_copy(i, peer).wait_send()
        for i in range(n_aux // 2):
            fock_copy(me_a, neighbour, i).wait_send()

    if_reducer(end_sends)
    for j, source in enumerate(near):

        def end_pass(source=source, j=j):
            fock_copy(source, neighbour, n_aux // 2 + j).wait_send()

        if chunks < n_aux:
            pl.when(me_a != source)(end_pass)
        elif j > 0:
            end_pass()


def finish(fock_in, gram_in, fock_out, gram_out, fock_v, gram_v, in_sem, out_sem):
    owned = fock_in.shape[0]
    legs = [(fock_in.at[k], fock_v.at[k], fock_out.at[k]) for k in range(owned)]
    legs.append((gram_in, gram_v, gram_out))
    inward = [pltpu.make_async_copy(a, v, in_sem.at[i]) for i, (a, v, _) in enumerate(legs)]
    outward = [pltpu.make_async_copy(v, b, out_sem.at[i]) for i, (_, v, b) in enumerate(legs)]
    for copy in inward:
        copy.start()
    for arrive, leave in zip(inward, outward):
        arrive.wait()
        leave.start()
    for copy in outward:
        copy.wait()


def shards(three_centre, block_mask, block_owner, block_index, active_orbitals, inactive_orbitals):
    slots, rows, width, _ = three_centre.shape
    n_aux = lax.axis_size("aux")
    n_pair = lax.axis_size("pair")
    act = active_orbitals.shape[0]
    blocks = active_orbitals.shape[1] // width
    pairs = act * act
    act_pad = -(-act // 16) * 16
    chunk_rows = max(16, width // n_aux)
    chunks = width // chunk_rows
    parts = 2
    part_pad = -(-(rows // parts) // 16) * 16
    owned = n_pair * slots // 2
    dma = pltpu.SemaphoreType.DMA
    vmem = pl.BlockSpec(memory_space=pltpu.VMEM)
    hbm = pl.BlockSpec(memory_space=pltpu.HBM)
    fock, gram = pl.pallas_call(
        functools.partial(kernel, n_aux, n_pair),
        out_shape=(
            jax.ShapeDtypeStruct((owned, width, width), F32),
            jax.ShapeDtypeStruct((pairs // n_aux, pairs), F32),
        ),
        in_specs=[hbm] * 6,
        out_specs=(vmem, vmem),
        scratch_shapes=[
            pltpu.SMEM(block_mask.shape, jnp.int32),
            pltpu.SMEM(block_owner.shape, jnp.int32),
            pltpu.SMEM(block_index.shape, jnp.int32),
            pltpu.VMEM(active_orbitals.shape, BF16),
            pltpu.VMEM(three_centre.shape, BF16),
            pltpu.VMEM((blocks, inactive_orbitals.shape[0], width), BF16),
            pltpu.VMEM((blocks, act, width), F32),
            pltpu.VMEM((rows, 8, width), F32),
            pltpu.VMEM((n_pair, rows, width), F32),
            pltpu.VMEM((rows, width), F32),
            pltpu.VMEM((rows, act_pad, slots * width), BF16),
            pltpu.VMEM((pairs, slots * width), BF16),
            pltpu.VMEM((parts, part_pad, pairs), F32),
            pltpu.VMEM((n_pair, part_pad, pairs), F32),
            pltpu.VMEM((parts, n_aux, part_pad, pairs), BF16),
            pltpu.VMEM((chunks, slots, chunk_rows, width), BF16),
            pltpu.VMEM((n_aux, slots, chunk_rows, width), BF16),
            pltpu.VMEM((n_pair * slots, chunk_rows, width), BF16),
            pltpu.VMEM((chunks, owned, chunk_rows, width), BF16),
            dma((4,)),
            dma((slots,)),
            dma((blocks,)),
            dma((n_pair,)),
            dma((n_pair,)),
            dma((n_pair,)),
            dma((n_pair,)),
            dma((slots, chunks)),
            dma((slots, n_aux)),
            dma((n_aux,)),
            dma((n_aux,)),
            dma,
            dma,
            dma((n_pair,)),
            dma((n_pair,)),
            dma((n_aux,)),
            dma((chunks,)),
        ],
        compiler_params=pltpu.CompilerParams(
            collective_id=0, has_side_effects=True, vmem_limit_bytes=60 * 1024 * 1024
        ),
    )(
        three_centre,
        block_mask,
        block_owner,
        block_index,
        active_orbitals,
        inactive_orbitals,
    )
    return pl.pallas_call(
        finish,
        out_shape=(
            jax.ShapeDtypeStruct(fock.shape, F32),
            jax.ShapeDtypeStruct(gram.shape, F32),
        ),
        in_specs=[hbm, hbm],
        out_specs=(hbm, hbm),
        scratch_shapes=[
            pltpu.VMEM(fock.shape, F32),
            pltpu.VMEM(gram.shape, F32),
            dma((owned + 1,)),
            dma((owned + 1,)),
        ],
        compiler_params=pltpu.CompilerParams(vmem_limit_bytes=60 * 1024 * 1024),
    )(fock, gram)


def solution(mesh):
    return jax.shard_map(
        shards,
        mesh=mesh,
        in_specs=(P("pair", "aux", None, None), P(), P(), P(), P(), P()),
        out_specs=(P("pair", None, None), P("aux", None)),
        check_vma=False,
    )
```
